32 devices in a mesh: rep: 16 (over z, x, core), ctx: 2 (over y).
Axes of the slice: x: 2, y: 2, z: 4, core: 2. Of those that a mesh axis runs over, the one named last changes fastest.
Arguments:
- activations: bfloat16 [16, 256, 4096], P('rep', 'ctx'), may hold values from -6 to 6
- queries: bfloat16 [16, 256, 2048], P('rep', 'ctx'), may hold values from -110 to 110
- key_states: bfloat16 [16, 256, 512], P('rep', 'ctx'), may hold values from -4 to 4
- targets: bfloat16 [16, 256, 2048], P('rep', 'ctx'), may hold values from -1.5 to 1.5
- value_weight: bfloat16 [16, 4096, 512], P('rep', 'ctx'), may hold values from -5 to 5
- tracker: bfloat16 [16, 4096, 512], P('rep', 'ctx'), may hold values from -5 to 5
- old_gradient: bfloat16 [16, 4096, 512], P('rep', 'ctx'), may hold values from -5 to 5
Outputs:
- new_weight: bfloat16 [16, 4096, 512], P('rep', 'ctx')
- new_tracker: bfloat16 [16, 4096, 512], P('rep', 'ctx')
The draws below stay inside these ranges and needn't reach their ends.
All inputs are finite; a program needn't handle non-finite values.
Results may differ from the reference program's by a relative error of at most 0.0095.
Values may be sent and summed in bfloat16 or wider, within the bound.
No kernel may reach another device: no remote copies, remote signals or barrier semaphores. Data moves between devices by JAX's collectives and lax.ppermute only.
A program may use at most 64 MiB of HBM per device.

```python
import jax
import jax.numpy as jnp
from jax import lax

D = 4096
HEADS = 16
KV_HEADS = 4
HEAD_DIM = 128
ROUND = 3
SEQ = 256
N_REP = 16


def paired_draw(key):
    base = jax.random.fold_in(key, 17)
    key_part, query_part = jax.random.split(base)
    key_rows = jax.random.truncated_normal(key_part, -4.0, 4.0, (N_REP, SEQ, KV_HEADS * HEAD_DIM), jnp.float32)
    query_rows = jax.random.truncated_normal(query_part, -4.0, 4.0, (N_REP, SEQ, HEADS * HEAD_DIM), jnp.float32)
    return (query_rows, key_rows)


def draw_queries(key, part):
    return paired_draw(key)[0].astype(jnp.bfloat16)


def draw_key_states(key, part):
    return paired_draw(key)[1].astype(jnp.bfloat16)


def block_levels(stream_key, extent, cuts, least, largest):
    level = 1.0
    for dim, shards_of in cuts:
        draws = jax.random.uniform(jax.random.fold_in(jax.random.fold_in(stream_key, 6), dim), (shards_of,), jnp.float32, least / len(cuts), largest / len(cuts))
        level = level * jnp.repeat(jnp.exp(draws), extent[dim] // shards_of).reshape((-1,) + (1,) * (len(extent) - 1 - dim))
    return level


def noise(own_key, dims, width, reach, shards=(), held_as=jnp.bfloat16):
    level = block_levels(own_key, dims, shards, -0.22, 0.18) if shards else 1.0
    entries = jax.random.normal(own_key, dims, jnp.float32) * width * level
    return jnp.minimum(jnp.maximum(entries, -reach), reach).astype(held_as)


def setup_inputs(seed: int = 0) -> dict:
    keys = jax.random.split(jax.random.key(seed), 8)
    activations = noise(keys[0], (N_REP, SEQ, D), 1.0, 6.0, ((0, 16), (1, 2)))
    queries = draw_queries(jax.random.fold_in(keys[7], 71), 0)
    key_states = draw_key_states(jax.random.fold_in(keys[7], 71), 0)
    targets = noise(keys[3], (N_REP, SEQ, HEADS * HEAD_DIM), 0.25, 1.5, ((0, 16), (1, 2)))
    value_weight = noise(keys[4], (N_REP, D, KV_HEADS * HEAD_DIM), 1.0, 5.0, ((0, 16), (1, 2)))
    tracker = noise(keys[5], (N_REP, D, KV_HEADS * HEAD_DIM), 1.0, 5.0, ((0, 16), (1, 2)))
    old_gradient = noise(keys[6], (N_REP, D, KV_HEADS * HEAD_DIM), 1.0, 5.0, ((0, 16), (1, 2)))
    return dict(activations=activations, queries=queries, key_states=key_states, targets=targets, value_weight=value_weight, tracker=tracker, old_gradient=old_gradient)


step_size = 0.25
loss_weight = 16.0


def replica_round(operands):
    activations, queries, key_states, targets, weight, tracker, old_gradient = operands
    value_scale = D ** -0.5
    grouping = HEADS // KV_HEADS
    values = (jnp.dot(activations, weight, preferred_element_type=jnp.float32) * value_scale).astype(jnp.bfloat16)
    query_heads = queries.astype(jnp.float32).reshape(SEQ, KV_HEADS, grouping, HEAD_DIM)
    key_heads = key_states.astype(jnp.float32).reshape(SEQ, KV_HEADS, HEAD_DIM)
    value_heads = values.astype(jnp.float32).reshape(SEQ, KV_HEADS, HEAD_DIM)
    scores = jnp.einsum("ikgd,jkd->kgij", query_heads, key_heads) * (HEAD_DIM ** -0.5)
    positions = jnp.arange(SEQ)
    allowed = positions[None, :] <= positions[:, None]
    scores = jnp.where(allowed, scores, -jnp.inf)
    highest = jnp.max(scores, axis=-1, keepdims=True)
    raised = jnp.exp(scores - highest)
    probabilities = (raised / jnp.sum(raised, axis=-1, keepdims=True)).astype(jnp.bfloat16)
    prob_full = probabilities.astype(jnp.float32)
    attended = jnp.einsum("kgij,jkd->ikgd", prob_full, value_heads).reshape(SEQ, HEADS * HEAD_DIM)
    out_cot = (loss_weight * (attended - targets.astype(jnp.float32))).astype(jnp.bfloat16)
    cot_heads = out_cot.astype(jnp.float32).reshape(SEQ, KV_HEADS, grouping, HEAD_DIM)
    value_cot = jnp.einsum("kgij,ikgd->jkd", prob_full, cot_heads).reshape(SEQ, KV_HEADS * HEAD_DIM)
    value_cot16 = value_cot.astype(jnp.bfloat16)
    gradient = jnp.dot(activations.T, value_cot16, preferred_element_type=jnp.float32) * value_scale
    tracker_half = tracker.astype(jnp.float32) + gradient - old_gradient.astype(jnp.float32)
    moved = weight.astype(jnp.float32) - step_size * tracker_half
    return moved, tracker_half


def reference(activations, queries, key_states, targets, value_weight, tracker, old_gradient):
    moved, tracker_half = lax.map(replica_round, (activations, queries, key_states, targets, value_weight, tracker, old_gradient))
    partner = jnp.bitwise_xor(jnp.arange(N_REP, dtype=jnp.int32), jnp.int32(2 ** ROUND))
    new_weight = ((moved + moved[partner]) * 0.5).astype(jnp.bfloat16)
    new_tracker = ((tracker_half + tracker_half[partner]) * 0.5).astype(jnp.bfloat16)
    return new_weight, new_tracker
```

```python
import functools

import jax
import jax.numpy as jnp
from jax import lax
from jax.experimental import pallas as pl
from jax.experimental.pallas import tpu as pltpu
from jax.sharding import PartitionSpec as P

HEADS = 16
KV_HEADS = 4
HEAD_DIM = 128
ROUND = 3
GROUP = HEADS // KV_HEADS

STEP_SIZE = 0.25
LOSS_WEIGHT = 16.0
CHUNKS = 4
ROWS = 256
VMEM = 32 * 1024 * 1024


def params(**more):
    return pltpu.CompilerParams(vmem_limit_bytes=VMEM, **more)


def shift(block, by):
    n = lax.axis_size("ctx")
    return lax.ppermute(block, "ctx", [(i, (i + by) % n) for i in range(n)])


def partner(block):
    n = lax.axis_size("rep")
    return lax.ppermute(block, "rep", [(i, i ^ 1 << ROUND) for i in range(n)])


def stack_heads(block):
    return jnp.concatenate([block[:, g * HEAD_DIM : (g + 1) * HEAD_DIM] for g in range(GROUP)], axis=0)


def probs_kernel(n, me_ref, q_ref, *refs):
    key_refs, out_ref = refs[:n], refs[n]
    tokens = q_ref.shape[0]
    keys = jnp.concatenate([k[...] for k in key_refs], axis=0)
    scores = lax.dot_general(
        stack_heads(q_ref[...]), keys, (((1,), (1,)), ((), ())), preferred_element_type=jnp.float32
    ) * HEAD_DIM ** (-0.5)
    scores = scores.reshape(GROUP, tokens, n * tokens)
    row = lax.broadcasted_iota(jnp.int32, scores.shape, 1)
    col = lax.broadcasted_iota(jnp.int32, scores.shape, 2)
    last = jnp.where(col < tokens, row, (me_ref[0] + 1) * tokens - 1)
    scores = jnp.where(col <= last, scores, -jnp.inf)
    highest = jnp.max(scores, axis=-1, keepdims=True)
    raised = jnp.exp(scores - highest)
    out_ref[...] = (raised / jnp.sum(raised, axis=-1, keepdims=True)).astype(jnp.bfloat16)


def probabilities(me, queries, keys):
    n, (tokens, _) = len(keys), queries.shape
    return pl.pallas_call(
        functools.partial(probs_kernel, n),
        grid=(KV_HEADS,),
        in_specs=[
            pl.BlockSpec(memory_space=pltpu.SMEM),
            pl.BlockSpec((tokens, GROUP * HEAD_DIM), lambda k: (0, k)),
        ]
        + [pl.BlockSpec((tokens, HEAD_DIM), lambda k: (0, k))] * n,
        out_specs=pl.BlockSpec((GROUP, tokens, n * tokens), lambda k: (k, 0, 0)),
        out_shape=jax.ShapeDtypeStruct((HEADS, tokens, n * tokens), jnp.bfloat16),
        compiler_params=params(),
        cost_estimate=pl.CostEstimate(flops=2 * tokens * tokens * n * HEADS * HEAD_DIM, bytes_accessed=1 << 22, transcendentals=0),
        name="probabilities",
    )(me, queries, *keys)


def terms_kernel(n, probs_ref, target_ref, *refs):
    value_refs, out_refs = refs[:n], refs[n:]
    tokens = target_ref.shape[0]
    probs = probs_ref[...].reshape(GROUP * tokens, n * tokens)
    values = jnp.concatenate([v[...] for v in value_refs], axis=0)
    attended = jnp.dot(probs, values, preferred_element_type=jnp.float32)
    targets = stack_heads(target_ref[...]).astype(jnp.float32)
    cot = (LOSS_WEIGHT * (attended - targets)).astype(jnp.bfloat16)
    terms = lax.dot_general(probs, cot, (((0,), (0,)), ((), ())), preferred_element_type=jnp.float32)
    for s in range(n):
        out_refs[s][...] = terms[s * tokens : (s + 1) * tokens]


def value_terms(probs, targets, values):
    n, (tokens, _) = len(values), targets.shape
    block = pl.BlockSpec((tokens, HEAD_DIM), lambda k: (0, k))
    return pl.pallas_call(
        functools.partial(terms_kernel, n),
        grid=(KV_HEADS,),
        in_specs=[
            pl.BlockSpec((GROUP, tokens, n * tokens), lambda k: (k, 0, 0)),
            pl.BlockSpec((tokens, GROUP * HEAD_DIM), lambda k: (0, k)),
        ]
        + [block] * n,
        out_specs=[block] * n,
        out_shape=[jax.ShapeDtypeStruct((tokens, KV_HEADS * HEAD_DIM), jnp.float32)] * n,
        compiler_params=params(),
        cost_estimate=pl.CostEstimate(flops=4 * tokens * tokens * n * HEADS * HEAD_DIM, bytes_accessed=1 << 22, transcendentals=0),
        name="value_terms",
    )(probs, targets, *values)


def tracker_kernel(n, scale, track_ref, old_ref, *refs):
    feature_refs, cot_refs, (wide_ref, sent_ref) = refs[:n], refs[n : 2 * n], refs[2 * n : 2 * n + 2]
    gradient = sum(
        lax.dot_general(f[...], c[...], (((0,), (0,)), ((), ())), preferred_element_type=jnp.float32)
        for f, c in zip(feature_refs, cot_refs)
    )
    half = track_ref[...].astype(jnp.float32) + gradient * scale - old_ref[...].astype(jnp.float32)
    wide_ref[...] = half
    sent_ref[...] = half.astype(jnp.bfloat16)


def tracker_chunk(chunk, rows, scale, track, old, features, cots, after):
    n, (tokens, _) = len(features), features[0].shape
    cols = track.shape[1]
    step = min(ROWS, rows)
    first = chunk * (rows // step)
    moving = pl.BlockSpec((step, cols), lambda i: (first + i, 0))
    own = pl.BlockSpec((step, cols), lambda i: (i, 0))
    return pl.pallas_call(
        functools.partial(tracker_kernel, n, scale),
        grid=(rows // step,),
        in_specs=[moving, moving]
        + [pl.BlockSpec((tokens, step), lambda i: (0, first + i))] * n
        + [pl.BlockSpec((tokens, cols), lambda i: (0, 0))] * n,
        out_specs=[own, own],
        out_shape=[
            jax.ShapeDtypeStruct((rows, cols), jnp.float32),
            jax.ShapeDtypeStruct((rows, cols), jnp.bfloat16),
        ],
        compiler_params=params(),
        cost_estimate=pl.CostEstimate(flops=2 * rows * tokens * n * cols, bytes_accessed=10 * rows * cols, transcendentals=0),
        name="tracker_half",
    )(track, old, *features, *cots)


def mix_kernel(weight_ref, peer_weight_ref, half_ref, peer_half_ref, *refs):
    new_weight_ref, new_tracker_ref = refs[-2:]
    both = half_ref[...] + peer_half_ref[...].astype(jnp.float32)
    weights = weight_ref[...].astype(jnp.float32) + peer_weight_ref[...].astype(jnp.float32)
    new_weight_ref[...] = ((weights - STEP_SIZE * both) * 0.5).astype(jnp.bfloat16)
    new_tracker_ref[...] = (both * 0.5).astype(jnp.bfloat16)


def mix_chunk(chunk, weight, peer_weight, half, peer_half, outs):
    rows, cols = half.shape
    step = min(ROWS, rows)
    first = chunk * (rows // step)
    moving = pl.BlockSpec((step, cols), lambda i: (first + i, 0))
    own = pl.BlockSpec((step, cols), lambda i: (i, 0))
    return pl.pallas_call(
        mix_kernel,
        grid=(rows // step,),
        in_specs=[moving, moving, own, own] + [pl.BlockSpec(memory_space=pl.ANY)] * len(outs),
        out_specs=[moving, moving],
        out_shape=[jax.ShapeDtypeStruct(weight.shape, jnp.bfloat16)] * 2,
        input_output_aliases={4 + i: i for i in range(len(outs))},
        compiler_params=params(),
        cost_estimate=pl.CostEstimate(flops=5 * rows * cols, bytes_accessed=14 * rows * cols, transcendentals=0),
        name="mix",
    )(weight, peer_weight, half, peer_half, *outs)


def local(activations, queries, key_states, targets, value_weight, tracker, old_gradient):
    n, me = lax.axis_size("ctx"), lax.axis_index("ctx")
    tokens, width = activations.shape[1:]
    scale = width ** (-0.5)
    depth = width // n
    weight = value_weight[0]
    peer_weight = partner(weight)

    columns = [lax.dynamic_slice_in_dim(activations[0], (me + s) % n * depth, depth, axis=1) for s in range(n)]
    features = [columns[0]] + [shift(columns[s], s) for s in range(1, n)]
    keys = [key_states[0]] + [shift(key_states[0], s) for s in range(1, n)]
    probs = probabilities(me.astype(jnp.int32).reshape(1), queries[0], keys)

    parts = [jnp.dot(f, weight, preferred_element_type=jnp.float32) for f in features]
    own = parts[0] + sum(shift(parts[s], -s) for s in range(1, n))
    own_values = (own * scale).astype(jnp.bfloat16)
    values = [own_values] + [shift(own_values, s) for s in range(1, n)]

    terms = value_terms(probs, targets[0], values)
    own_cot = (terms[0] + sum(shift(terms[s], -s) for s in range(1, n))).astype(jnp.bfloat16)
    cots = [own_cot] + [shift(own_cot, s) for s in range(1, n)]

    rows = depth // CHUNKS
    outs = ()
    for c in range(CHUNKS):
        half, sent = tracker_chunk(c, rows, scale, tracker[0], old_gradient[0], features, cots, None)
        outs = mix_chunk(c, weight, peer_weight, half, partner(sent), outs)
    return outs[0][None], outs[1][None]


def solution(mesh):
    spec = P("rep", "ctx", None)
    return jax.shard_map(
        local,
        mesh=mesh,
        in_specs=(spec,) * 7,
        out_specs=(spec, spec),
        check_vma=False,
    )
```

```python
import functools

import jax
import jax.numpy as jnp
from jax import lax
from jax.experimental import pallas as pl
from jax.experimental.pallas import tpu as pltpu
from jax.sharding import PartitionSpec as P

HEADS = 16
KV_HEADS = 4
HEAD_DIM = 128
ROUND = 3
GROUP = HEADS // KV_HEADS

STEP_SIZE = 0.25
LOSS_WEIGHT = 16.0
CHUNKS = 4
ROWS = 256
VMEM = 32 * 1024 * 1024


def params(**more):
    return pltpu.CompilerParams(vmem_limit_bytes=VMEM, **more)


def shift(block, by):
    n = lax.axis_size("ctx")
    return lax.ppermute(block, "ctx", [(i, (i + by) % n) for i in range(n)])


def partner(block):
    n = lax.axis_size("rep")
    return lax.ppermute(block, "rep", [(i, i ^ 1 << ROUND) for i in range(n)])


def stack_heads(block):
    return jnp.concatenate([block[:, g * HEAD_DIM : (g + 1) * HEAD_DIM] for g in range(GROUP)], axis=0)


def probs_kernel(n, me_ref, q_ref, *refs):
    key_refs, out_ref = refs[:n], refs[n]
    tokens = q_ref.shape[0]
    keys = jnp.concatenate([k[...] for k in key_refs], axis=0)
    scores = lax.dot_general(
        stack_heads(q_ref[...]), keys, (((1,), (1,)), ((), ())), preferred_element_type=jnp.float32
    ) * HEAD_DIM ** (-0.5)
    scores = scores.reshape(GROUP, tokens, n * tokens)
    row = lax.broadcasted_iota(jnp.int32, scores.shape, 1)
    col = lax.broadcasted_iota(jnp.int32, scores.shape, 2)
    last = jnp.where(col < tokens, row, (me_ref[0] + 1) * tokens - 1)
    scores = jnp.where(col <= last, scores, -jnp.inf)
    highest = jnp.max(scores, axis=-1, keepdims=True)
    raised = jnp.exp(scores - highest)
    out_ref[...] = (raised / jnp.sum(raised, axis=-1, keepdims=True)).astype(jnp.bfloat16)


def probabilities(me, queries, keys):
    n, (tokens, _) = len(keys), queries.shape
    return pl.pallas_call(
        functools.partial(probs_kernel, n),
        grid=(KV_HEADS,),
        in_specs=[
            pl.BlockSpec(memory_space=pltpu.SMEM),
            pl.BlockSpec((tokens, GROUP * HEAD_DIM), lambda k: (0, k)),
        ]
        + [pl.BlockSpec((tokens, HEAD_DIM), lambda k: (0, k))] * n,
        out_specs=pl.BlockSpec((GROUP, tokens, n * tokens), lambda k: (k, 0, 0)),
        out_shape=jax.ShapeDtypeStruct((HEADS, tokens, n * tokens), jnp.bfloat16),
        compiler_params=params(),
        cost_estimate=pl.CostEstimate(flops=2 * tokens * tokens * n * HEADS * HEAD_DIM, bytes_accessed=1 << 22, transcendentals=0),
        name="probabilities",
    )(me, queries, *keys)


def terms_kernel(n, probs_ref, target_ref, *refs):
    value_refs, out_refs = refs[:n], refs[n:]
    tokens = target_ref.shape[0]
    probs = probs_ref[...].reshape(GROUP * tokens, n * tokens)
    values = jnp.concatenate([v[...] for v in value_refs], axis=0)
    attended = jnp.dot(probs, values, preferred_element_type=jnp.float32)
    targets = stack_heads(target_ref[...]).astype(jnp.float32)
    cot = (LOSS_WEIGHT * (attended - targets)).astype(jnp.bfloat16)
    terms = lax.dot_general(probs, cot, (((0,), (0,)), ((), ())), preferred_element_type=jnp.float32)
    for s in range(n):
        out_refs[s][...] = terms[s * tokens : (s + 1) * tokens]


def value_terms(probs, targets, values):
    n, (tokens, _) = len(values), targets.shape
    block = pl.BlockSpec((tokens, HEAD_DIM), lambda k: (0, k))
    return pl.pallas_call(
        functools.partial(terms_kernel, n),
        grid=(KV_HEADS,),
        in_specs=[
            pl.BlockSpec((GROUP, tokens, n * tokens), lambda k: (k, 0, 0)),
            pl.BlockSpec((tokens, GROUP * HEAD_DIM), lambda k: (0, k)),
        ]
        + [block] * n,
        out_specs=[block] * n,
        out_shape=[jax.ShapeDtypeStruct((tokens, KV_HEADS * HEAD_DIM), jnp.float32)] * n,
        compiler_params=params(),
        cost_estimate=pl.CostEstimate(flops=4 * tokens * tokens * n * HEADS * HEAD_DIM, bytes_accessed=1 << 22, transcendentals=0),
        name="value_terms",
    )(probs, targets, *values)


def tracker_kernel(n, scale, track_ref, old_ref, *refs):
    feature_refs, cot_refs, (wide_ref, sent_ref) = refs[:n], refs[n : 2 * n], refs[2 * n : 2 * n + 2]
    gradient = sum(
        lax.dot_general(f[...], c[...], (((0,), (0,)), ((), ())), preferred_element_type=jnp.float32)
        for f, c in zip(feature_refs, cot_refs)
    )
    half = track_ref[...].astype(jnp.float32) + gradient * scale - old_ref[...].astype(jnp.float32)
    wide_ref[...] = half
    sent_ref[...] = half.astype(jnp.bfloat16)


def tracker_chunk(chunk, rows, scale, track, old, features, cots, after):
    n, (tokens, _) = len(features), features[0].shape
    cols = track.shape[1]
    step = min(ROWS, rows)
    first = chunk * (rows // step)
    moving = pl.BlockSpec((step, cols), lambda i: (first + i, 0))
    own = pl.BlockSpec((step, cols), lambda i: (i, 0))
    return pl.pallas_call(
        functools.partial(tracker_kernel, n, scale),
        grid=(rows // step,),
        in_specs=[moving, moving]
        + [pl.BlockSpec((tokens, step), lambda i: (0, first + i))] * n
        + [pl.BlockSpec((tokens, cols), lambda i: (0, 0))] * n,
        out_specs=[own, own],
        out_shape=[
            jax.ShapeDtypeStruct((rows, cols), jnp.float32),
            jax.ShapeDtypeStruct((rows, cols), jnp.bfloat16),
        ],
        compiler_params=params(),
        cost_estimate=pl.CostEstimate(flops=2 * rows * tokens * n * cols, bytes_accessed=10 * rows * cols, transcendentals=0),
        name="tracker_half",
    )(track, old, *features, *cots)


def mix_kernel(weight_ref, peer_weight_ref, half_ref, peer_half_ref, *refs):
    new_weight_ref, new_tracker_ref = refs[-2:]
    both = half_ref[...] + peer_half_ref[...].astype(jnp.float32)
    weights = weight_ref[...].astype(jnp.float32) + peer_weight_ref[...].astype(jnp.float32)
    new_weight_ref[...] = ((weights - STEP_SIZE * both) * 0.5).astype(jnp.bfloat16)
    new_tracker_ref[...] = (both * 0.5).astype(jnp.bfloat16)


def mix_chunk(chunk, weight, peer_weight, half, peer_half, outs):
    rows, cols = half.shape
    step = min(ROWS, rows)
    first = chunk * (rows // step)
    moving = pl.BlockSpec((step, cols), lambda i: (first + i, 0))
    own = pl.BlockSpec((step, cols), lambda i: (i, 0))
    return pl.pallas_call(
        mix_kernel,
        grid=(rows // step,),
        in_specs=[moving, moving, own, own] + [pl.BlockSpec(memory_space=pl.ANY)] * len(outs),
        out_specs=[moving, moving],
        out_shape=[jax.ShapeDtypeStruct(weight.shape, jnp.bfloat16)] * 2,
        input_output_aliases={4 + i: i for i in range(len(outs))},
        compiler_params=params(),
        cost_estimate=pl.CostEstimate(flops=5 * rows * cols, bytes_accessed=14 * rows * cols, transcendentals=0),
        name="mix",
    )(weight, peer_weight, half, peer_half, *outs)


def local(activations, queries, key_states, targets, value_weight, tracker, old_gradient):
    n, me = lax.axis_size("ctx"), lax.axis_index("ctx")
    tokens, width = activations.shape[1:]
    scale = width ** (-0.5)
    depth = width // n
    weight = value_weight[0]
    peer_weight = partner(weight)

    def chain():
        columns = [lax.dynamic_slice_in_dim(activations[0], (me + s) % n * depth, depth, axis=1) for s in range(n)]
        features = [columns[0]] + [shift(columns[s], s) for s in range(1, n)]
        keys = [key_states[0]] + [shift(key_states[0], s) for s in range(1, n)]
        probs = probabilities(me.astype(jnp.int32).reshape(1), queries[0], keys)

        parts = [jnp.dot(f, weight, preferred_element_type=jnp.float32) for f in features]
        own = parts[0] + sum(shift(parts[s], -s) for s in range(1, n))
        own_values = (own * scale).astype(jnp.bfloat16)
        values = [own_values] + [shift(own_values, s) for s in range(1, n)]

        terms = value_terms(probs, targets[0], values)
        own_cot = (terms[0] + sum(shift(terms[s], -s) for s in range(1, n))).astype(jnp.bfloat16)
        cots = [own_cot] + [shift(own_cot, s) for s in range(1, n)]
        return features, cots

    def never():
        shapes = jax.eval_shape(chain)
        return jax.tree.map(lambda x: jnp.zeros(x.shape, x.dtype), shapes)

    features, cots = lax.cond(me < n, chain, never)

    rows = depth // CHUNKS
    outs = ()
    for c in range(CHUNKS):
        half, sent = tracker_chunk(c, rows, scale, tracker[0], old_gradient[0], features, cots, None)
        outs = mix_chunk(c, weight, peer_weight, half, partner(sent), outs)
    return outs[0][None], outs[1][None]


def solution(mesh):
    spec = P("rep", "ctx", None)
    return jax.shard_map(
        local,
        mesh=mesh,
        in_specs=(spec,) * 7,
        out_specs=(spec, spec),
        check_vma=False,
    )
```

```python
import functools
import math

import jax
import jax.numpy as jnp
from jax import lax
from jax.experimental import pallas as pl
from jax.experimental.pallas import tpu as pltpu
from jax.sharding import PartitionSpec as P

HEADS = 16
KV_HEADS = 4
HEAD_DIM = 128
ROUND = 3
GROUP = HEADS // KV_HEADS

STEP_SIZE = 0.25
LOSS_WEIGHT = 16.0
SHARES = (5, 5, 5, 1)
ROWS = 256
LANES = 128
VMEM = 32 * 1024 * 1024


def params(**more):
    return pltpu.CompilerParams(vmem_limit_bytes=VMEM, **more)


def shift(block, by):
    n = lax.axis_size("ctx")
    return lax.ppermute(block, "ctx", [(i, (i + by) % n) for i in range(n)])


def partner(block):
    n = lax.axis_size("rep")
    return lax.ppermute(block, "rep", [(i, i ^ 1 << ROUND) for i in range(n)])


def stack_heads(block):
    return jnp.concatenate([block[:, g * HEAD_DIM : (g + 1) * HEAD_DIM] for g in range(GROUP)], axis=0)


def probs_kernel(n, me_ref, q_ref, *refs):
    key_refs, out_ref = refs[:n], refs[n]
    tokens = q_ref.shape[0]
    keys = jnp.concatenate([k[...] for k in key_refs], axis=0)
    scores = lax.dot_general(
        stack_heads(q_ref[...]), keys, (((1,), (1,)), ((), ())), preferred_element_type=jnp.float32
    ) * HEAD_DIM ** (-0.5)
    scores = scores.reshape(GROUP, tokens, n * tokens)
    row = lax.broadcasted_iota(jnp.int32, scores.shape, 1)
    col = lax.broadcasted_iota(jnp.int32, scores.shape, 2)
    last = jnp.where(col < tokens, row, (me_ref[0] + 1) * tokens - 1)
    scores = jnp.where(col <= last, scores, -jnp.inf)
    highest = jnp.max(scores, axis=-1, keepdims=True)
    raised = jnp.exp(scores - highest)
    out_ref[...] = (raised / jnp.sum(raised, axis=-1, keepdims=True)).astype(jnp.bfloat16)


def probabilities(me, queries, keys):
    n, (tokens, _) = len(keys), queries.shape
    return pl.pallas_call(
        functools.partial(probs_kernel, n),
        grid=(KV_HEADS,),
        in_specs=[
            pl.BlockSpec(memory_space=pltpu.SMEM),
            pl.BlockSpec((tokens, GROUP * HEAD_DIM), lambda k: (0, k)),
        ]
        + [pl.BlockSpec((tokens, HEAD_DIM), lambda k: (0, k))] * n,
        out_specs=pl.BlockSpec((GROUP, tokens, n * tokens), lambda k: (k, 0, 0)),
        out_shape=jax.ShapeDtypeStruct((HEADS, tokens, n * tokens), jnp.bfloat16),
        compiler_params=params(),
        cost_estimate=pl.CostEstimate(flops=2 * tokens * tokens * n * HEADS * HEAD_DIM, bytes_accessed=1 << 22, transcendentals=0),
        name="probabilities",
    )(me, queries, *keys)


def terms_kernel(n, probs_ref, target_ref, *refs):
    value_refs, out_refs = refs[:n], refs[n:]
    tokens = target_ref.shape[0]
    probs = probs_ref[...].reshape(GROUP * tokens, n * tokens)
    values = jnp.concatenate([v[...] for v in value_refs], axis=0)
    attended = jnp.dot(probs, values, preferred_element_type=jnp.float32)
    targets = stack_heads(target_ref[...]).astype(jnp.float32)
    cot = (LOSS_WEIGHT * (attended - targets)).astype(jnp.bfloat16)
    terms = lax.dot_general(probs, cot, (((0,), (0,)), ((), ())), preferred_element_type=jnp.float32)
    for s in range(n):
        out_refs[s][...] = terms[s * tokens : (s + 1) * tokens]


def value_terms(probs, targets, values):
    n, (tokens, _) = len(values), targets.shape
    block = pl.BlockSpec((tokens, HEAD_DIM), lambda k: (0, k))
    return pl.pallas_call(
        functools.partial(terms_kernel, n),
        grid=(KV_HEADS,),
        in_specs=[
            pl.BlockSpec((GROUP, tokens, n * tokens), lambda k: (k, 0, 0)),
            pl.BlockSpec((tokens, GROUP * HEAD_DIM), lambda k: (0, k)),
        ]
        + [block] * n,
        out_specs=[block] * n,
        out_shape=[jax.ShapeDtypeStruct((tokens, KV_HEADS * HEAD_DIM), jnp.float32)] * n,
        compiler_params=params(),
        cost_estimate=pl.CostEstimate(flops=4 * tokens * tokens * n * HEADS * HEAD_DIM, bytes_accessed=1 << 22, transcendentals=0),
        name="value_terms",
    )(probs, targets, *values)


def tracker_kernel(n, scale, track_ref, old_ref, *refs):
    feature_refs, cot_refs, (wide_ref, sent_ref) = refs[:n], refs[n : 2 * n], refs[2 * n : 2 * n + 2]
    gradient = sum(
        lax.dot_general(f[...], c[...], (((0,), (0,)), ((), ())), preferred_element_type=jnp.float32)
        for f, c in zip(feature_refs, cot_refs)
    )
    half = track_ref[...].astype(jnp.float32) + gradient * scale - old_ref[...].astype(jnp.float32)
    wide_ref[...] = half
    sent_ref[...] = half.astype(jnp.bfloat16)


def tracker_chunk(start, rows, scale, track, old, features, cots):
    n, (tokens, _) = len(features), features[0].shape
    cols = track.shape[1]
    step = math.gcd(start, rows, ROWS)
    first = start // step
    moving = pl.BlockSpec((step, cols), lambda i: (first + i, 0))
    own = pl.BlockSpec((step, cols), lambda i: (i, 0))
    return pl.pallas_call(
        functools.partial(tracker_kernel, n, scale),
        grid=(rows // step,),
        in_specs=[moving, moving]
        + [pl.BlockSpec((tokens, step), lambda i: (0, first + i))] * n
        + [pl.BlockSpec((tokens, cols), lambda i: (0, 0))] * n,
        out_specs=[own, own],
        out_shape=[
            jax.ShapeDtypeStruct((rows, cols), jnp.float32),
            jax.ShapeDtypeStruct((rows, cols), jnp.bfloat16),
        ],
        compiler_params=params(),
        cost_estimate=pl.CostEstimate(flops=2 * rows * tokens * n * cols, bytes_accessed=10 * rows * cols, transcendentals=0),
        name="tracker_half",
    )(track, old, *features, *cots)


def mix_kernel(start, weight_ref, peer_weight_ref, half_ref, peer_half_ref, *refs):
    *_, new_weight_ref, new_tracker_ref, weight_out, tracker_out, sems = refs
    copies = []
    for slab in range(half_ref.shape[0] // LANES):
        here = pl.ds(slab * LANES, LANES)
        there = pl.ds(start + slab * LANES, LANES)
        both = half_ref[here] + peer_half_ref[here].astype(jnp.float32)
        weights = weight_ref[there].astype(jnp.float32) + peer_weight_ref[there].astype(jnp.float32)
        weight_out[here] = ((weights - STEP_SIZE * both) * 0.5).astype(jnp.bfloat16)
        tracker_out[here] = (both * 0.5).astype(jnp.bfloat16)
        for i, (out, ref) in enumerate(((weight_out, new_weight_ref), (tracker_out, new_tracker_ref))):
            copies.append(pltpu.make_async_copy(out.at[here], ref.at[there], sems.at[i, slab]))
            copies[-1].start()
    for copy in copies:
        copy.wait()


def mix_chunk(start, weight, peer_weight, half, peer_half, outs):
    rows, cols = half.shape
    return pl.pallas_call(
        functools.partial(mix_kernel, start),
        in_specs=[pl.BlockSpec(memory_space=pltpu.VMEM)] * 4 + [pl.BlockSpec(memory_space=pl.ANY)] * len(outs),
        out_specs=[pl.BlockSpec(memory_space=pl.ANY)] * 2,
        out_shape=[jax.ShapeDtypeStruct(weight.shape, jnp.bfloat16)] * 2,
        scratch_shapes=[pltpu.VMEM((rows, cols), jnp.bfloat16)] * 2
        + [pltpu.SemaphoreType.DMA((2, rows // LANES))],
        input_output_aliases={4 + i: i for i in range(len(outs))},
        compiler_params=params(),
        cost_estimate=pl.CostEstimate(flops=5 * rows * cols, bytes_accessed=14 * rows * cols, transcendentals=0),
        name="mix",
    )(weight, peer_weight, half, peer_half, *outs)


def local(activations, queries, key_states, targets, value_weight, tracker, old_gradient):
    n, me = lax.axis_size("ctx"), lax.axis_index("ctx")
    tokens, width = activations.shape[1:]
    scale = width ** (-0.5)
    depth = width // n
    weight = value_weight[0]
    peer_weight = partner(weight)

    def chain():
        columns = [lax.dynamic_slice_in_dim(activations[0], (me + s) % n * depth, depth, axis=1) for s in range(n)]
        features = [columns[0]] + [shift(columns[s], s) for s in range(1, n)]
        keys = [key_states[0]] + [shift(key_states[0], s) for s in range(1, n)]
        probs = probabilities(me.astype(jnp.int32).reshape(1), queries[0], keys)

        parts = [jnp.dot(f, weight, preferred_element_type=jnp.float32) for f in features]
        own = parts[0] + sum(shift(parts[s], -s) for s in range(1, n))
        own_values = (own * scale).astype(jnp.bfloat16)
        values = [own_values] + [shift(own_values, s) for s in range(1, n)]

        terms = value_terms(probs, targets[0], values)
        own_cot = (terms[0] + sum(shift(terms[s], -s) for s in range(1, n))).astype(jnp.bfloat16)
        cots = [own_cot] + [shift(own_cot, s) for s in range(1, n)]
        return features, cots

    def never():
        shapes = jax.eval_shape(chain)
        return jax.tree.map(lambda x: jnp.zeros(x.shape, x.dtype), shapes)

    features, cots = lax.cond(me < n, chain, never)

    units = depth // LANES
    cuts = [units * sum(SHARES[:c]) // sum(SHARES) * LANES for c in range(len(SHARES) + 1)]
    outs = ()
    for start, end in zip(cuts, cuts[1:]):
        if start == end:
            continue
        half, sent = tracker_chunk(start, end - start, scale, tracker[0], old_gradient[0], features, cots)
        outs = mix_chunk(start, weight, peer_weight, half, partner(sent), outs)
    return outs[0][None], outs[1][None]


def solution(mesh):
    spec = P("rep", "ctx", None)
    return jax.shard_map(
        local,
        mesh=mesh,
        in_specs=(spec,) * 7,
        out_specs=(spec, spec),
        check_vma=False,
    )
```

```python
import functools
import math

import jax
import jax.numpy as jnp
from jax import lax
from jax.experimental import pallas as pl
from jax.experimental.pallas import tpu as pltpu
from jax.sharding import PartitionSpec as P

HEADS = 16
KV_HEADS = 4
HEAD_DIM = 128
ROUND = 3
GROUP = HEADS // KV_HEADS

STEP_SIZE = 0.25
LOSS_WEIGHT = 16.0
SHARES = (5, 5, 5, 1)
ROWS = 256
LANES = 128
VMEM = 32 * 1024 * 1024


def params(**more):
    return pltpu.CompilerParams(vmem_limit_bytes=VMEM, **more)


def shift(block, by):
    n = lax.axis_size("ctx")
    return lax.ppermute(block, "ctx", [(i, (i + by) % n) for i in range(n)])


def partner(block):
    n = lax.axis_size("rep")
    return lax.ppermute(block, "rep", [(i, i ^ 1 << ROUND) for i in range(n)])


def stack_heads(block):
    return jnp.concatenate([block[:, g * HEAD_DIM : (g + 1) * HEAD_DIM] for g in range(GROUP)], axis=0)


def probs_kernel(n, me_ref, q_ref, *refs):
    key_refs, out_ref = refs[:n], refs[n]
    tokens = q_ref.shape[0]
    keys = jnp.concatenate([k[...] for k in key_refs], axis=0)
    scores = lax.dot_general(
        stack_heads(q_ref[...]), keys, (((1,), (1,)), ((), ())), preferred_element_type=jnp.float32
    ) * HEAD_DIM ** (-0.5)
    scores = scores.reshape(GROUP, tokens, n * tokens)
    row = lax.broadcasted_iota(jnp.int32, scores.shape, 1)
    col = lax.broadcasted_iota(jnp.int32, scores.shape, 2)
    last = jnp.where(col < tokens, row, (me_ref[0] + 1) * tokens - 1)
    scores = jnp.where(col <= last, scores, -jnp.inf)
    highest = jnp.max(scores, axis=-1, keepdims=True)
    raised = jnp.exp(scores - highest)
    out_ref[...] = (raised / jnp.sum(raised, axis=-1, keepdims=True)).astype(jnp.bfloat16)


def probabilities(me, queries, keys):
    n, (tokens, _) = len(keys), queries.shape
    return pl.pallas_call(
        functools.partial(probs_kernel, n),
        grid=(KV_HEADS,),
        in_specs=[
            pl.BlockSpec(memory_space=pltpu.SMEM),
            pl.BlockSpec((tokens, GROUP * HEAD_DIM), lambda k: (0, k)),
        ]
        + [pl.BlockSpec((tokens, HEAD_DIM), lambda k: (0, k))] * n,
        out_specs=pl.BlockSpec((GROUP, tokens, n * tokens), lambda k: (k, 0, 0)),
        out_shape=jax.ShapeDtypeStruct((HEADS, tokens, n * tokens), jnp.bfloat16),
        compiler_params=params(),
        cost_estimate=pl.CostEstimate(flops=2 * tokens * tokens * n * HEADS * HEAD_DIM, bytes_accessed=1 << 22, transcendentals=0),
        name="probabilities",
    )(me, queries, *keys)


def terms_kernel(n, probs_ref, target_ref, *refs):
    value_refs, out_refs = refs[:n], refs[n:]
    tokens = target_ref.shape[0]
    probs = probs_ref[...].reshape(GROUP * tokens, n * tokens)
    values = jnp.concatenate([v[...] for v in value_refs], axis=0)
    attended = jnp.dot(probs, values, preferred_element_type=jnp.float32)
    targets = stack_heads(target_ref[...]).astype(jnp.float32)
    cot = (LOSS_WEIGHT * (attended - targets)).astype(jnp.bfloat16)
    terms = lax.dot_general(probs, cot, (((0,), (0,)), ((), ())), preferred_element_type=jnp.float32)
    for s in range(n):
        out_refs[s][...] = terms[s * tokens : (s + 1) * tokens]


def value_terms(probs, targets, values):
    n, (tokens, _) = len(values), targets.shape
    block = pl.BlockSpec((tokens, HEAD_DIM), lambda k: (0, k))
    return pl.pallas_call(
        functools.partial(terms_kernel, n),
        grid=(KV_HEADS,),
        in_specs=[
            pl.BlockSpec((GROUP, tokens, n * tokens), lambda k: (k, 0, 0)),
            pl.BlockSpec((tokens, GROUP * HEAD_DIM), lambda k: (0, k)),
        ]
        + [block] * n,
        out_specs=[block] * n,
        out_shape=[jax.ShapeDtypeStruct((tokens, KV_HEADS * HEAD_DIM), jnp.float32)] * n,
        compiler_params=params(),
        cost_estimate=pl.CostEstimate(flops=4 * tokens * tokens * n * HEADS * HEAD_DIM, bytes_accessed=1 << 22, transcendentals=0),
        name="value_terms",
    )(probs, targets, *values)


def tracker_kernel(n, scale, track_ref, old_ref, *refs):
    feature_refs, cot_refs, (wide_ref, sent_ref) = refs[:n], refs[n : 2 * n], refs[-2:]
    gradient = sum(
        lax.dot_general(f[...], c[...], (((0,), (0,)), ((), ())), preferred_element_type=jnp.float32)
        for f, c in zip(feature_refs, cot_refs)
    )
    half = track_ref[...].astype(jnp.float32) + gradient * scale - old_ref[...].astype(jnp.float32)
    wide_ref[...] = half
    sent_ref[...] = half.astype(jnp.bfloat16)


def tracker_chunk(start, rows, scale, track, old, features, cots, after):
    n, (tokens, _) = len(features), features[0].shape
    cols = track.shape[1]
    step = math.gcd(start, rows, ROWS)
    first = start // step
    moving = pl.BlockSpec((step, cols), lambda i: (first + i, 0))
    own = pl.BlockSpec((step, cols), lambda i: (i, 0))
    return pl.pallas_call(
        functools.partial(tracker_kernel, n, scale),
        grid=(rows // step,),
        in_specs=[moving, moving]
        + [pl.BlockSpec((tokens, step), lambda i: (0, first + i))] * n
        + [pl.BlockSpec((tokens, cols), lambda i: (0, 0))] * n
        + [pl.BlockSpec(memory_space=pl.ANY)] * len(after),
        out_specs=[own, own],
        out_shape=[
            jax.ShapeDtypeStruct((rows, cols), jnp.float32),
            jax.ShapeDtypeStruct((rows, cols), jnp.bfloat16),
        ],
        compiler_params=params(),
        cost_estimate=pl.CostEstimate(flops=2 * rows * tokens * n * cols, bytes_accessed=10 * rows * cols, transcendentals=0),
        name="tracker_half",
    )(track, old, *features, *cots, *after)


def mix_kernel(start, weight_ref, peer_weight_ref, half_ref, peer_half_ref, *refs):
    *_, new_weight_ref, new_tracker_ref, weight_out, tracker_out, sems = refs
    copies = []
    for slab in range(half_ref.shape[0] // LANES):
        here = pl.ds(slab * LANES, LANES)
        there = pl.ds(start + slab * LANES, LANES)
        both = half_ref[here] + peer_half_ref[here].astype(jnp.float32)
        weights = weight_ref[there].astype(jnp.float32) + peer_weight_ref[there].astype(jnp.float32)
        weight_out[here] = ((weights - STEP_SIZE * both) * 0.5).astype(jnp.bfloat16)
        tracker_out[here] = (both * 0.5).astype(jnp.bfloat16)
        for i, (out, ref) in enumerate(((weight_out, new_weight_ref), (tracker_out, new_tracker_ref))):
            copies.append(pltpu.make_async_copy(out.at[here], ref.at[there], sems.at[i, slab]))
            copies[-1].start()
    for copy in copies:
        copy.wait()


def mix_chunk(start, weight, peer_weight, half, peer_half, outs):
    rows, cols = half.shape
    return pl.pallas_call(
        functools.partial(mix_kernel, start),
        in_specs=[pl.BlockSpec(memory_space=pltpu.VMEM)] * 4 + [pl.BlockSpec(memory_space=pl.ANY)] * len(outs),
        out_specs=[pl.BlockSpec(memory_space=pl.ANY)] * 2,
        out_shape=[jax.ShapeDtypeStruct(weight.shape, jnp.bfloat16)] * 2,
        scratch_shapes=[pltpu.VMEM((rows, cols), jnp.bfloat16)] * 2
        + [pltpu.SemaphoreType.DMA((2, rows // LANES))],
        input_output_aliases={4 + i: i for i in range(len(outs))},
        compiler_params=params(),
        cost_estimate=pl.CostEstimate(flops=5 * rows * cols, bytes_accessed=14 * rows * cols, transcendentals=0),
        name="mix",
    )(weight, peer_weight, half, peer_half, *outs)


def local(activations, queries, key_states, targets, value_weight, tracker, old_gradient):
    n, me = lax.axis_size("ctx"), lax.axis_index("ctx")
    tokens, width = activations.shape[1:]
    scale = width ** (-0.5)
    depth = width // n
    weight = value_weight[0]
    peer_weight = partner(weight)

    def chain():
        columns = [lax.dynamic_slice_in_dim(activations[0], (me + s) % n * depth, depth, axis=1) for s in range(n)]
        features = [columns[0]] + [shift(columns[s], s) for s in range(1, n)]
        keys = [key_states[0]] + [shift(key_states[0], s) for s in range(1, n)]
        probs = probabilities(me.astype(jnp.int32).reshape(1), queries[0], keys)

        parts = [jnp.dot(f, weight, preferred_element_type=jnp.float32) for f in features]
        own = parts[0] + sum(shift(parts[s], -s) for s in range(1, n))
        own_values = (own * scale).astype(jnp.bfloat16)
        values = [own_values] + [shift(own_values, s) for s in range(1, n)]

        terms = value_terms(probs, targets[0], values)
        own_cot = (terms[0] + sum(shift(terms[s], -s) for s in range(1, n))).astype(jnp.bfloat16)
        cots = [own_cot] + [shift(own_cot, s) for s in range(1, n)]
        return features, cots

    def never():
        shapes = jax.eval_shape(chain)
        return jax.tree.map(lambda x: jnp.zeros(x.shape, x.dtype), shapes)

    features, cots = lax.cond(me < n, chain, never)

    units = depth // LANES
    cuts = [units * sum(SHARES[:c]) // sum(SHARES) * LANES for c in range(len(SHARES) + 1)]
    outs = ()
    for start, end in zip(cuts, cuts[1:]):
        if start == end:
            continue
        after = [peer_weight] if start else []
        half, sent = tracker_chunk(start, end - start, scale, tracker[0], old_gradient[0], features, cots, after)
        outs = mix_chunk(start, weight, peer_weight, half, partner(sent), outs)
    return outs[0][None], outs[1][None]


def solution(mesh):
    spec = P("rep", "ctx", None)
    return jax.shard_map(
        local,
        mesh=mesh,
        in_specs=(spec,) * 7,
        out_specs=(spec, spec),
        check_vma=False,
    )
```

```python
import functools
import math

import jax
import jax.numpy as jnp
from jax import lax
from jax.experimental import pallas as pl
from jax.experimental.pallas import tpu as pltpu
from jax.sharding import PartitionSpec as P

HEADS = 16
KV_HEADS = 4
HEAD_DIM = 128
ROUND = 3
GROUP = HEADS // KV_HEADS

STEP_SIZE = 0.25
LOSS_WEIGHT = 16.0
SHARES = (5, 5, 5, 1)
ROWS = 256
LANES = 128
VMEM = 32 * 1024 * 1024


def params(**more):
    return pltpu.CompilerParams(vmem_limit_bytes=VMEM, **more)


def shift(block, by):
    n = lax.axis_size("ctx")
    return lax.ppermute(block, "ctx", [(i, (i + by) % n) for i in range(n)])


def partner(block):
    n = lax.axis_size("rep")
    return lax.ppermute(block, "rep", [(i, i ^ 1 << ROUND) for i in range(n)])


def stack_heads(block):
    return jnp.concatenate([block[:, g * HEAD_DIM : (g + 1) * HEAD_DIM] for g in range(GROUP)], axis=0)


def probs_kernel(n, me_ref, q_ref, *refs):
    key_refs, out_ref = refs[:n], refs[n]
    tokens = q_ref.shape[0]
    keys = jnp.concatenate([k[...] for k in key_refs], axis=0)
    scores = lax.dot_general(
        stack_heads(q_ref[...]), keys, (((1,), (1,)), ((), ())), preferred_element_type=jnp.float32
    ) * HEAD_DIM ** (-0.5)
    scores = scores.reshape(GROUP, tokens, n * tokens)
    row = lax.broadcasted_iota(jnp.int32, scores.shape, 1)
    col = lax.broadcasted_iota(jnp.int32, scores.shape, 2)
    last = jnp.where(col < tokens, row, (me_ref[0] + 1) * tokens - 1)
    scores = jnp.where(col <= last, scores, -jnp.inf)
    highest = jnp.max(scores, axis=-1, keepdims=True)
    raised = jnp.exp(scores - highest)
    out_ref[...] = (raised / jnp.sum(raised, axis=-1, keepdims=True)).astype(jnp.bfloat16)


def probabilities(me, queries, keys):
    n, (tokens, _) = len(keys), queries.shape
    return pl.pallas_call(
        functools.partial(probs_kernel, n),
        grid=(KV_HEADS,),
        in_specs=[
            pl.BlockSpec(memory_space=pltpu.SMEM),
            pl.BlockSpec((tokens, GROUP * HEAD_DIM), lambda k: (0, k)),
        ]
        + [pl.BlockSpec((tokens, HEAD_DIM), lambda k: (0, k))] * n,
        out_specs=pl.BlockSpec((GROUP, tokens, n * tokens), lambda k: (k, 0, 0)),
        out_shape=jax.ShapeDtypeStruct((HEADS, tokens, n * tokens), jnp.bfloat16),
        compiler_params=params(),
        cost_estimate=pl.CostEstimate(flops=2 * tokens * tokens * n * HEADS * HEAD_DIM, bytes_accessed=1 << 22, transcendentals=0),
        name="probabilities",
    )(me, queries, *keys)


def terms_kernel(n, probs_ref, target_ref, *refs):
    value_refs, out_refs = refs[:n], refs[n:]
    tokens = target_ref.shape[0]
    probs = probs_ref[...].reshape(GROUP * tokens, n * tokens)
    values = jnp.concatenate([v[...] for v in value_refs], axis=0)
    attended = jnp.dot(probs, values, preferred_element_type=jnp.float32)
    targets = stack_heads(target_ref[...]).astype(jnp.float32)
    cot = (LOSS_WEIGHT * (attended - targets)).astype(jnp.bfloat16)
    terms = lax.dot_general(probs, cot, (((0,), (0,)), ((), ())), preferred_element_type=jnp.float32)
    for s in range(n):
        out_refs[s][...] = terms[s * tokens : (s + 1) * tokens]


def value_terms(probs, targets, values):
    n, (tokens, _) = len(values), targets.shape
    block = pl.BlockSpec((tokens, HEAD_DIM), lambda k: (0, k))
    return pl.pallas_call(
        functools.partial(terms_kernel, n),
        grid=(KV_HEADS,),
        in_specs=[
            pl.BlockSpec((GROUP, tokens, n * tokens), lambda k: (k, 0, 0)),
            pl.BlockSpec((tokens, GROUP * HEAD_DIM), lambda k: (0, k)),
        ]
        + [block] * n,
        out_specs=[block] * n,
        out_shape=[jax.ShapeDtypeStruct((tokens, KV_HEADS * HEAD_DIM), jnp.float32)] * n,
        compiler_params=params(),
        cost_estimate=pl.CostEstimate(flops=4 * tokens * tokens * n * HEADS * HEAD_DIM, bytes_accessed=1 << 22, transcendentals=0),
        name="value_terms",
    )(probs, targets, *values)


def tracker_kernel(n, scale, track_ref, old_ref, *refs):
    feature_refs, cot_refs, sent_ref = refs[:n], refs[n : 2 * n], refs[2 * n]
    gradient = sum(
        lax.dot_general(f[...], c[...], (((0,), (0,)), ((), ())), preferred_element_type=jnp.float32)
        for f, c in zip(feature_refs, cot_refs)
    )
    half = track_ref[...].astype(jnp.float32) + gradient * scale - old_ref[...].astype(jnp.float32)
    sent_ref[...] = half.astype(jnp.bfloat16)


def tracker_chunk(start, rows, scale, track, old, features, cots):
    n, (tokens, _) = len(features), features[0].shape
    cols = track.shape[1]
    step = math.gcd(start, rows, ROWS)
    first = start // step
    moving = pl.BlockSpec((step, cols), lambda i: (first + i, 0))
    own = pl.BlockSpec((step, cols), lambda i: (i, 0))
    return pl.pallas_call(
        functools.partial(tracker_kernel, n, scale),
        grid=(rows // step,),
        in_specs=[moving, moving]
        + [pl.BlockSpec((tokens, step), lambda i: (0, first + i))] * n
        + [pl.BlockSpec((tokens, cols), lambda i: (0, 0))] * n,
        out_specs=own,
        out_shape=jax.ShapeDtypeStruct((rows, cols), jnp.bfloat16),
        compiler_params=params(),
        cost_estimate=pl.CostEstimate(flops=2 * rows * tokens * n * cols, bytes_accessed=6 * rows * cols, transcendentals=0),
        name="tracker_half",
    )(track, old, *features, *cots)


def mix_kernel(start, weight_ref, peer_weight_ref, half_ref, peer_half_ref, *refs):
    *_, new_weight_ref, new_tracker_ref, weight_out, tracker_out, sems = refs
    copies = []
    for slab in range(half_ref.shape[0] // LANES):
        here = pl.ds(slab * LANES, LANES)
        there = pl.ds(start + slab * LANES, LANES)
        both = half_ref[here].astype(jnp.float32) + peer_half_ref[here].astype(jnp.float32)
        weights = weight_ref[there].astype(jnp.float32) + peer_weight_ref[there].astype(jnp.float32)
        weight_out[here] = ((weights - STEP_SIZE * both) * 0.5).astype(jnp.bfloat16)
        tracker_out[here] = (both * 0.5).astype(jnp.bfloat16)
        for i, (out, ref) in enumerate(((weight_out, new_weight_ref), (tracker_out, new_tracker_ref))):
            copies.append(pltpu.make_async_copy(out.at[here], ref.at[there], sems.at[i, slab]))
            copies[-1].start()
    for copy in copies:
        copy.wait()


def mix_chunk(start, weight, peer_weight, half, peer_half, outs):
    rows, cols = half.shape
    return pl.pallas_call(
        functools.partial(mix_kernel, start),
        in_specs=[pl.BlockSpec(memory_space=pltpu.VMEM)] * 4 + [pl.BlockSpec(memory_space=pl.ANY)] * len(outs),
        out_specs=[pl.BlockSpec(memory_space=pl.ANY)] * 2,
        out_shape=[jax.ShapeDtypeStruct(weight.shape, jnp.bfloat16)] * 2,
        scratch_shapes=[pltpu.VMEM((rows, cols), jnp.bfloat16)] * 2
        + [pltpu.SemaphoreType.DMA((2, rows // LANES))],
        input_output_aliases={4 + i: i for i in range(len(outs))},
        compiler_params=params(),
        cost_estimate=pl.CostEstimate(flops=5 * rows * cols, bytes_accessed=12 * rows * cols, transcendentals=0),
        name="mix",
    )(weight, peer_weight, half, peer_half, *outs)


def local(activations, queries, key_states, targets, value_weight, tracker, old_gradient):
    n, me = lax.axis_size("ctx"), lax.axis_index("ctx")
    tokens, width = activations.shape[1:]
    scale = width ** (-0.5)
    depth = width // n
    weight = value_weight[0]
    peer_weight = partner(weight)

    def chain():
        columns = [lax.dynamic_slice_in_dim(activations[0], (me + s) % n * depth, depth, axis=1) for s in range(n)]
        features = [columns[0]] + [shift(columns[s], s) for s in range(1, n)]
        keys = [key_states[0]] + [shift(key_states[0], s) for s in range(1, n)]
        probs = probabilities(me.astype(jnp.int32).reshape(1), queries[0], keys)

        parts = [jnp.dot(f, weight, preferred_element_type=jnp.float32) for f in features]
        own = parts[0] + sum(shift(parts[s], -s) for s in range(1, n))
        own_values = (own * scale).astype(jnp.bfloat16)
        values = [own_values] + [shift(own_values, s) for s in range(1, n)]

        terms = value_terms(probs, targets[0], values)
        own_cot = (terms[0] + sum(shift(terms[s], -s) for s in range(1, n))).astype(jnp.bfloat16)
        cots = [own_cot] + [shift(own_cot, s) for s in range(1, n)]
        return features, cots

    def never():
        shapes = jax.eval_shape(chain)
        return jax.tree.map(lambda x: jnp.zeros(x.shape, x.dtype), shapes)

    features, cots = lax.cond(me < n, chain, never)

    units = depth // LANES
    cuts = [units * sum(SHARES[:c]) // sum(SHARES) * LANES for c in range(len(SHARES) + 1)]
    outs = ()
    for start, end in zip(cuts, cuts[1:]):
        if start == end:
            continue
        half = tracker_chunk(start, end - start, scale, tracker[0], old_gradient[0], features, cots)
        outs = mix_chunk(start, weight, peer_weight, half, partner(half), outs)
    return outs[0][None], outs[1][None]


def solution(mesh):
    spec = P("rep", "ctx", None)
    return jax.shard_map(
        local,
        mesh=mesh,
        in_specs=(spec,) * 7,
        out_specs=(spec, spec),
        check_vma=False,
    )
```

```python
import functools
import math

import jax
import jax.numpy as jnp
from jax import lax
from jax.experimental import pallas as pl
from jax.experimental.pallas import tpu as pltpu
from jax.sharding import PartitionSpec as P

HEADS = 16
KV_HEADS = 4
HEAD_DIM = 128
ROUND = 3
GROUP = HEADS // KV_HEADS

STEP_SIZE = 0.25
LOSS_WEIGHT = 16.0
SHARES = (5, 5, 5, 1)
ROWS = 256
LANES = 128
SLAB = 64
VMEM = 32 * 1024 * 1024


def params(**more):
    return pltpu.CompilerParams(vmem_limit_bytes=VMEM, **more)


def shift(block, by):
    n = lax.axis_size("ctx")
    return lax.ppermute(block, "ctx", [(i, (i + by) % n) for i in range(n)])


def partner(block):
    n = lax.axis_size("rep")
    return lax.ppermute(block, "rep", [(i, i ^ 1 << ROUND) for i in range(n)])


def stack_heads(block):
    return jnp.concatenate([block[:, g * HEAD_DIM : (g + 1) * HEAD_DIM] for g in range(GROUP)], axis=0)


def probs_kernel(n, me_ref, q_ref, *refs):
    key_refs, out_ref = refs[:n], refs[n]
    tokens = q_ref.shape[0]
    keys = jnp.concatenate([k[...] for k in key_refs], axis=0)
    scores = lax.dot_general(
        stack_heads(q_ref[...]), keys, (((1,), (1,)), ((), ())), preferred_element_type=jnp.float32
    ) * HEAD_DIM ** (-0.5)
    scores = scores.reshape(GROUP, tokens, n * tokens)
    row = lax.broadcasted_iota(jnp.int32, scores.shape, 1)
    col = lax.broadcasted_iota(jnp.int32, scores.shape, 2)
    last = jnp.where(col < tokens, row, (me_ref[0] + 1) * tokens - 1)
    scores = jnp.where(col <= last, scores, -jnp.inf)
    highest = jnp.max(scores, axis=-1, keepdims=True)
    raised = jnp.exp(scores - highest)
    out_ref[...] = (raised / jnp.sum(raised, axis=-1, keepdims=True)).astype(jnp.bfloat16)


def probabilities(me, queries, keys):
    n, (tokens, _) = len(keys), queries.shape
    return pl.pallas_call(
        functools.partial(probs_kernel, n),
        grid=(KV_HEADS,),
        in_specs=[
            pl.BlockSpec(memory_space=pltpu.SMEM),
            pl.BlockSpec((tokens, GROUP * HEAD_DIM), lambda k: (0, k)),
        ]
        + [pl.BlockSpec((tokens, HEAD_DIM), lambda k: (0, k))] * n,
        out_specs=pl.BlockSpec((GROUP, tokens, n * tokens), lambda k: (k, 0, 0)),
        out_shape=jax.ShapeDtypeStruct((HEADS, tokens, n * tokens), jnp.bfloat16),
        compiler_params=params(),
        cost_estimate=pl.CostEstimate(flops=2 * tokens * tokens * n * HEADS * HEAD_DIM, bytes_accessed=1 << 22, transcendentals=0),
        name="probabilities",
    )(me, queries, *keys)


def terms_kernel(n, probs_ref, target_ref, *refs):
    value_refs, out_refs = refs[:n], refs[n:]
    tokens = target_ref.shape[0]
    probs = probs_ref[...].reshape(GROUP * tokens, n * tokens)
    values = jnp.concatenate([v[...] for v in value_refs], axis=0)
    attended = jnp.dot(probs, values, preferred_element_type=jnp.float32)
    targets = stack_heads(target_ref[...]).astype(jnp.float32)
    cot = (LOSS_WEIGHT * (attended - targets)).astype(jnp.bfloat16)
    terms = lax.dot_general(probs, cot, (((0,), (0,)), ((), ())), preferred_element_type=jnp.float32)
    for s in range(n):
        out_refs[s][...] = terms[s * tokens : (s + 1) * tokens]


def value_terms(probs, targets, values):
    n, (tokens, _) = len(values), targets.shape
    block = pl.BlockSpec((tokens, HEAD_DIM), lambda k: (0, k))
    return pl.pallas_call(
        functools.partial(terms_kernel, n),
        grid=(KV_HEADS,),
        in_specs=[
            pl.BlockSpec((GROUP, tokens, n * tokens), lambda k: (k, 0, 0)),
            pl.BlockSpec((tokens, GROUP * HEAD_DIM), lambda k: (0, k)),
        ]
        + [block] * n,
        out_specs=[block] * n,
        out_shape=[jax.ShapeDtypeStruct((tokens, KV_HEADS * HEAD_DIM), jnp.float32)] * n,
        compiler_params=params(),
        cost_estimate=pl.CostEstimate(flops=4 * tokens * tokens * n * HEADS * HEAD_DIM, bytes_accessed=1 << 22, transcendentals=0),
        name="value_terms",
    )(probs, targets, *values)


def tracker_kernel(n, scale, track_ref, old_ref, *refs):
    feature_refs, cot_refs, (wide_ref, sent_ref) = refs[:n], refs[n : 2 * n], refs[2 * n : 2 * n + 2]
    gradient = sum(
        lax.dot_general(f[...], c[...], (((0,), (0,)), ((), ())), preferred_element_type=jnp.float32)
        for f, c in zip(feature_refs, cot_refs)
    )
    half = track_ref[...].astype(jnp.float32) + gradient * scale - old_ref[...].astype(jnp.float32)
    wide_ref[...] = half
    sent_ref[...] = half.astype(jnp.bfloat16)


def tracker_chunk(start, rows, scale, track, old, features, cots):
    n, (tokens, _) = len(features), features[0].shape
    cols = track.shape[1]
    step = math.gcd(start, rows, ROWS)
    first = start // step
    moving = pl.BlockSpec((step, cols), lambda i: (first + i, 0))
    own = pl.BlockSpec((step, cols), lambda i: (i, 0))
    return pl.pallas_call(
        functools.partial(tracker_kernel, n, scale),
        grid=(rows // step,),
        in_specs=[moving, moving]
        + [pl.BlockSpec((tokens, step), lambda i: (0, first + i))] * n
        + [pl.BlockSpec((tokens, cols), lambda i: (0, 0))] * n,
        out_specs=[own, own],
        out_shape=[
            jax.ShapeDtypeStruct((rows, cols), jnp.float32),
            jax.ShapeDtypeStruct((rows, cols), jnp.bfloat16),
        ],
        compiler_params=params(),
        cost_estimate=pl.CostEstimate(flops=2 * rows * tokens * n * cols, bytes_accessed=10 * rows * cols, transcendentals=0),
        name="tracker_half",
    )(track, old, *features, *cots)


def mix_kernel(start, weight_ref, peer_weight_ref, half_ref, peer_half_ref, *refs):
    *_, new_weight_ref, new_tracker_ref, weight_out, tracker_out, sems = refs
    copies = []
    for slab in range(half_ref.shape[0] // SLAB):
        here = pl.ds(slab * SLAB, SLAB)
        there = pl.ds(start + slab * SLAB, SLAB)
        both = half_ref[here] + peer_half_ref[here].astype(jnp.float32)
        weights = weight_ref[there].astype(jnp.float32) + peer_weight_ref[there].astype(jnp.float32)
        weight_out[here] = ((weights - STEP_SIZE * both) * 0.5).astype(jnp.bfloat16)
        tracker_out[here] = (both * 0.5).astype(jnp.bfloat16)
        for i, (out, ref) in enumerate(((weight_out, new_weight_ref), (tracker_out, new_tracker_ref))):
            copies.append(pltpu.make_async_copy(out.at[here], ref.at[there], sems.at[i, slab]))
            copies[-1].start()
    for copy in copies:
        copy.wait()


def mix_chunk(start, weight, peer_weight, half, peer_half, outs):
    rows, cols = half.shape
    return pl.pallas_call(
        functools.partial(mix_kernel, start),
        in_specs=[pl.BlockSpec(memory_space=pltpu.VMEM)] * 4 + [pl.BlockSpec(memory_space=pl.ANY)] * len(outs),
        out_specs=[pl.BlockSpec(memory_space=pl.ANY)] * 2,
        out_shape=[jax.ShapeDtypeStruct(weight.shape, jnp.bfloat16)] * 2,
        scratch_shapes=[pltpu.VMEM((rows, cols), jnp.bfloat16)] * 2
        + [pltpu.SemaphoreType.DMA((2, rows // SLAB))],
        input_output_aliases={4 + i: i for i in range(len(outs))},
        compiler_params=params(),
        cost_estimate=pl.CostEstimate(flops=5 * rows * cols, bytes_accessed=14 * rows * cols, transcendentals=0),
        name="mix",
    )(weight, peer_weight, half, peer_half, *outs)


def local(activations, queries, key_states, targets, value_weight, tracker, old_gradient):
    n, me = lax.axis_size("ctx"), lax.axis_index("ctx")
    tokens, width = activations.shape[1:]
    scale = width ** (-0.5)
    depth = width // n
    weight = value_weight[0]
    peer_weight = partner(weight)

    def chain():
        columns = [lax.dynamic_slice_in_dim(activations[0], (me + s) % n * depth, depth, axis=1) for s in range(n)]
        features = [columns[0]] + [shift(columns[s], s) for s in range(1, n)]
        keys = [key_states[0]] + [shift(key_states[0], s) for s in range(1, n)]
        probs = probabilities(me.astype(jnp.int32).reshape(1), queries[0], keys)

        parts = [jnp.dot(f, weight, preferred_element_type=jnp.float32) for f in features]
        own = parts[0] + sum(shift(parts[s], -s) for s in range(1, n))
        own_values = (own * scale).astype(jnp.bfloat16)
        values = [own_values] + [shift(own_values, s) for s in range(1, n)]

        terms = value_terms(probs, targets[0], values)
        own_cot = (terms[0] + sum(shift(terms[s], -s) for s in range(1, n))).astype(jnp.bfloat16)
        cots = [own_cot] + [shift(own_cot, s) for s in range(1, n)]
        return features, cots

    def never():
        shapes = jax.eval_shape(chain)
        return jax.tree.map(lambda x: jnp.zeros(x.shape, x.dtype), shapes)

    features, cots = lax.cond(me < n, chain, never)

    units = depth // LANES
    cuts = [units * sum(SHARES[:c]) // sum(SHARES) * LANES for c in range(len(SHARES) + 1)]
    outs = ()
    for start, end in zip(cuts, cuts[1:]):
        if start == end:
            continue
        half, sent = tracker_chunk(start, end - start, scale, tracker[0], old_gradient[0], features, cots)
        outs = mix_chunk(start, weight, peer_weight, half, partner(sent), outs)
    return outs[0][None], outs[1][None]


def solution(mesh):
    spec = P("rep", "ctx", None)
    return jax.shard_map(
        local,
        mesh=mesh,
        in_specs=(spec,) * 7,
        out_specs=(spec, spec),
        check_vma=False,
    )
```
